128 devices in a mesh: blk: 32 (over y, x_lo, z), grp: 4 (over x_hi, core).
Axes of the slice: x: 4 (x_hi: 2, x_lo: 2; x = x_hi * 2 + x_lo), y: 4, z: 4, core: 2. Of those that a mesh axis runs over, the one named last changes fastest.
Arguments:
- item_factors: bfloat16 [16384, 256], P('blk'), may hold values from -0.046875 to 0.046875
- exposure: bfloat16 [16384], P('blk'), may hold values from 0.05 to 0.9
- confidence: bfloat16 [128, 128, 128, 128], P(('blk', 'grp')), as said below
- tile_items: int32 [128, 128], P(('blk', 'grp')), may hold values from 0 to 127, as said below
- tile_users: int32 [128, 128], P(('blk', 'grp')), may hold values from 0 to 3, as said below
- tile_count: int32 [128], P(('blk', 'grp')), may hold values from 42 to 128, as said below
Outputs:
- user_factors: bfloat16 [65536, 256], P(('blk', 'grp'))
- item_update: bfloat16 [16384, 256], P(('blk', 'grp'))
- user_gram: float32 [256, 256], replicated
The draws below stay inside these ranges and needn't reach their ends.
Inputs may be any that keep to these rules, and one draw needn't show every extreme that they name: `tile_items`: row d names an item block for each of device d's 128 tiles, each of the 128 item blocks once; some item block is among the live tiles of every device. `tile_users`: every one of a device's 4 user blocks appears among its first 4 tiles. A device's live tiles are its first tile_count ones; some device has all 128 live. `confidence`: zero where the user has not seen the item, else 1 or more; in every tile each user row and each item column has an entry of 1 or more.
All inputs are finite; a program needn't handle non-finite values.
Results may differ from the reference program's by a relative error of at most 0.0055.
The reference program's roundings to bfloat16 on the way count: a program that leaves them out, or rounds other values in their place, can miss the bound.
Values may be sent and summed in bfloat16 or wider, within the bound.
No kernel may reach another device: no remote copies, remote signals or barrier semaphores. Data moves between devices by JAX's collectives and lax.ppermute only.
A program may use at most 192 MiB of HBM per device.

```python
import jax
import jax.numpy as jnp
from jax import lax

BS = 128
RANK = 256
UB_DEV = 4
CG_STEPS = 3
TILES = 128
ITEMS = 16384
USERS = 65536
DEVICES = 128


def draw_exposure(key, part):
    key = jax.random.fold_in(key, 9)
    places = jnp.arange(ITEMS, dtype=jnp.float32) / (ITEMS - 1)
    base = 0.2 * jnp.exp(places * jnp.log(4.5))
    rough = jnp.exp(jax.random.uniform(jax.random.fold_in(key, 1), (ITEMS,), minval=jnp.log(0.5), maxval=0.0))
    return (base * rough).astype(jnp.bfloat16)


def draw_tile_items(key, part):
    key = jax.random.fold_in(key, 5)
    favourite = jax.random.randint(jax.random.fold_in(key, 1), (), 0, TILES)
    popularity = jax.random.randint(jax.random.fold_in(key, 2), (TILES,), 0, 8192)
    owners = jnp.arange(TILES, dtype=jnp.int32)
    popularity = jnp.where(owners == favourite, 1 << 20, popularity)
    jitter = jax.random.randint(jax.random.fold_in(key, 3), (TILES, TILES), 0, 4096)
    ranking = (jitter + popularity[None, :]) * TILES + owners[None, :]
    return jnp.argsort(-ranking, axis=1).astype(jnp.int32)


def draw_tile_users(key, part):
    key = jax.random.fold_in(key, 6)
    offset = jax.random.randint(jax.random.fold_in(key, 1), (TILES, 1), 0, UB_DEV)
    places = jnp.arange(TILES, dtype=jnp.int32)[None, :]
    leading = (places + offset) % UB_DEV
    others = jax.random.randint(jax.random.fold_in(key, 2), (TILES, TILES), 0, UB_DEV)
    return jnp.where(places < UB_DEV, leading, others).astype(jnp.int32)


def draw_tile_count(key, part):
    key = jax.random.fold_in(key, 7)
    counts = jax.random.randint(jax.random.fold_in(key, 1), (TILES,), TILES // 3, TILES // 2 + 1)
    busiest = jax.random.randint(jax.random.fold_in(key, 2), (), 0, TILES)
    return jnp.where(jnp.arange(TILES, dtype=jnp.int32) == busiest, TILES, counts).astype(jnp.int32)


def draw_confidence(key, part):
    key = jax.random.fold_in(key, 8)
    extent = (TILES, TILES, BS, BS)
    observed = jax.random.uniform(jax.random.fold_in(key, 1), extent) < 0.5
    shifts = jax.random.randint(jax.random.fold_in(key, 4), (TILES, TILES, 1, 1), 0, BS)
    user_pos = jnp.arange(BS, dtype=jnp.int32)[:, None]
    item_pos = jnp.arange(BS, dtype=jnp.int32)[None, :]
    diagonal = user_pos == (item_pos + shifts) % BS
    observed = jnp.logical_or(observed, diagonal)
    strength = jnp.exp(jax.random.uniform(jax.random.fold_in(key, 2), extent, maxval=jnp.log(4.0)))
    return jnp.where(observed, strength, 0.0).astype(jnp.bfloat16)


def block_scale(key, dims, pieces, smallest, top_value):
    factor_of, own = 1.0, jax.random.fold_in(key, 6)
    for dim, shards_of in pieces:
        steps = jnp.exp(jax.random.uniform(jax.random.fold_in(own, dim), (shards_of,), jnp.float32, smallest / len(pieces), top_value / len(pieces)))
        factor_of = factor_of * jnp.repeat(steps, dims[dim] // shards_of).reshape([-1 if axis == dim else 1 for axis in range(len(dims))])
    return factor_of


def gaussian(rng, dims, spread, most, split=(), held_as=jnp.bfloat16):
    entries = spread * jax.random.normal(rng, dims, jnp.float32)
    if split:
        entries = entries * block_scale(rng, dims, split, -0.22, 0.18)
    return jnp.clip(entries, -most, most).astype(held_as)


def setup_inputs(seed: int = 0) -> dict:
    seeds = jax.random.split(jax.random.key(seed), 7)
    item_factors = gaussian(seeds[0], (ITEMS, RANK), ITEMS ** -0.5, 0.046875, ((0, 32),))
    exposure = draw_exposure(jax.random.fold_in(seeds[6], 71), 0)
    confidence = draw_confidence(jax.random.fold_in(seeds[6], 71), 0)
    tile_items = draw_tile_items(jax.random.fold_in(seeds[6], 71), 0)
    tile_users = draw_tile_users(jax.random.fold_in(seeds[6], 71), 0)
    tile_count = draw_tile_count(jax.random.fold_in(seeds[6], 71), 0)
    return dict(item_factors=item_factors, exposure=exposure, confidence=confidence, tile_items=tile_items, tile_users=tile_users, tile_count=tile_count)


LAMBDA = 1.0
FULL_PRECISION = lax.Precision.HIGHEST

def conjugate(right_side, operator, step_count):
    solution = jnp.zeros_like(right_side)
    residual = right_side
    direction = right_side
    norm_now = lax.optimization_barrier(jnp.sum(residual * residual, axis=1, keepdims=True))
    for iteration in range(step_count):
        mapped = operator(direction)
        stride = norm_now / lax.optimization_barrier(jnp.sum(direction * mapped, axis=1, keepdims=True))
        solution = solution + stride * direction
        residual = residual - stride * mapped
        norm_next = lax.optimization_barrier(jnp.sum(residual * residual, axis=1, keepdims=True))
        direction = residual + norm_next / norm_now * direction
        norm_now = norm_next
    return solution

def bf16_round(values):
    narrow = lax.optimization_barrier(values.astype(jnp.bfloat16))
    return narrow.astype(jnp.float32)

def reference(item_factors, exposure, confidence, tile_items, tile_users, tile_count):
    factor_wide = item_factors.astype(jnp.float32)
    exposure_wide = exposure.astype(jnp.float32)
    gram_items = jnp.dot((factor_wide * exposure_wide[:, None]).T, factor_wide, precision=FULL_PRECISION)
    offsets = jnp.arange(BS, dtype=jnp.int32)
    block_ids = jnp.arange(UB_DEV, dtype=jnp.int32)
    tile_ids = jnp.arange(TILES, dtype=jnp.int32)

    def user_device(inputs):
        conf_tiles, item_row, user_row, live_count = inputs
        item_index = item_row[:, None] * BS + offsets[None, :]
        tile_factors = factor_wide[item_index]
        tile_exposure = exposure_wide[item_index]
        active = tile_ids < live_count
        conf_live = jnp.where(active[:, None, None], conf_tiles.astype(jnp.float32), 0.0)
        excess = jnp.where(conf_live > 0, conf_live - tile_exposure[:, None, :], 0.0)
        member = (user_row[:, None] == block_ids[None, :]).astype(jnp.float32)
        tile_right = jnp.einsum('tui,tik->tuk', conf_live, tile_factors, precision=FULL_PRECISION)
        user_right = jnp.einsum('tb,tuk->buk', member, tile_right, precision=FULL_PRECISION).reshape(UB_DEV * BS, RANK)

        def operator(direction):
            rounded = bf16_round(direction).reshape(UB_DEV, BS, RANK)
            picked = rounded[user_row]
            scores = jnp.einsum('tuk,tik->tui', picked, tile_factors, precision=FULL_PRECISION)
            weighted = bf16_round(excess * scores)
            returned = jnp.einsum('tui,tik->tuk', weighted, tile_factors, precision=FULL_PRECISION)
            summed = jnp.einsum('tb,tuk->buk', member, returned, precision=FULL_PRECISION).reshape(UB_DEV * BS, RANK)
            return LAMBDA * direction + jnp.dot(direction, gram_items, precision=FULL_PRECISION) + summed
        return conjugate(user_right, operator, CG_STEPS)
    solved = lax.map(user_device, (confidence, tile_items, tile_users, tile_count))
    user_factors = solved.reshape(USERS, RANK).astype(jnp.bfloat16)
    gram_users = jnp.dot(user_factors.T, user_factors, preferred_element_type=jnp.float32)
    user_gram = gram_users * (1.0 / (UB_DEV * BS))
    user_wide = user_factors.astype(jnp.float32).reshape(DEVICES, UB_DEV, BS, RANK)
    device_ids = jnp.arange(DEVICES, dtype=jnp.int32)
    row_ids = jnp.broadcast_to(device_ids[:, None], (DEVICES, TILES))
    column_ids = jnp.broadcast_to(tile_ids[None, :], (DEVICES, TILES))
    position = jnp.zeros((DEVICES, TILES), jnp.int32).at[row_ids, tile_items].set(column_ids)

    def item_owner(owner_index):
        slot_index = position[:, owner_index]
        active = slot_index < tile_count
        conf_live = jnp.where(active[:, None, None], confidence[device_ids, slot_index].astype(jnp.float32), 0.0)
        user_block = tile_users[device_ids, slot_index]
        user_rows = jnp.where(active[:, None, None], user_wide[device_ids, user_block], 0.0)
        own_exposure = lax.dynamic_slice_in_dim(exposure_wide, owner_index * BS, BS)
        excess = jnp.where(conf_live > 0, conf_live - own_exposure[None, None, :], 0.0)
        item_right = jnp.einsum('sui,suk->ik', conf_live, user_rows, precision=FULL_PRECISION)

        def operator(direction):
            rounded = bf16_round(direction)
            scores = jnp.einsum('suk,ik->sui', user_rows, rounded, precision=FULL_PRECISION)
            weighted = bf16_round(excess * scores)
            returned = jnp.einsum('sui,suk->ik', weighted, user_rows, precision=FULL_PRECISION)
            gram_term = jnp.dot(direction, user_gram, precision=FULL_PRECISION)
            return LAMBDA * direction + own_exposure[:, None] * gram_term + returned
        return conjugate(item_right, operator, CG_STEPS)
    item_solved = lax.map(item_owner, device_ids)
    item_update = (item_solved.reshape(ITEMS, RANK) * math_sqrt_devices()).astype(jnp.bfloat16)
    return (user_factors, item_update, user_gram)

def math_sqrt_devices():
    return float(DEVICES) ** 0.5
```

```python
import functools

import jax
import jax.numpy as jnp
from jax import lax
from jax.experimental import pallas as pl
from jax.experimental.pallas import tpu as pltpu
from jax.sharding import PartitionSpec as P

UB = 4
BS = 128
RANK = 256
TILES = 128
STEPS = 3
GROUP = 4
SLOTS = TILES + UB * GROUP
HIGH = lax.Precision.HIGHEST
BF = jnp.bfloat16
F32 = jnp.float32
VMEM_BYTES = 56 * 1024 * 1024
BOTH = ("blk", "grp")


def nt(a, b):
    return lax.dot_general(a, b, (((1,), (1,)), ((), ())), preferred_element_type=F32)


def nn(a, b):
    return lax.dot_general(a, b, (((1,), (0,)), ((), ())), preferred_element_type=F32)


def tn(a, b):
    return lax.dot_general(a, b, (((0,), (0,)), ((), ())), preferred_element_type=F32)


def row_sum(v):
    return jnp.sum(v, axis=1, keepdims=True)


def send_kernel(items, count, conf, out):
    def one(t, carry):
        tile = conf[t]
        tile = jnp.where(t < count[0], tile, jnp.zeros_like(tile))
        out[items[t]] = tile.T
        return carry

    lax.fori_loop(0, TILES, one, 0, unroll=4)


def send_conf_of(items, count, conf):
    smem = pl.BlockSpec(memory_space=pltpu.SMEM)
    vmem = pl.BlockSpec(memory_space=pltpu.VMEM)
    return pl.pallas_call(
        send_kernel,
        out_shape=jax.ShapeDtypeStruct((TILES, BS, BS), BF),
        in_specs=[smem, smem, vmem],
        out_specs=vmem,
        compiler_params=pltpu.CompilerParams(vmem_limit_bytes=VMEM_BYTES),
        name="send_conf",
    )(items, count, conf)


def user_kernel(
    items, users, count, conf_hbm, factors_hbm, exposure,
    out, rows_hbm, gram_out,
    conf, factors, slots, heads, gram, right, direction, narrow, mapped, answer, residual, sems,
):
    conf_copy = pltpu.make_async_copy(conf_hbm, conf.at[pl.ds(0, TILES)], sems.at[0])
    factor_copy = pltpu.make_async_copy(factors_hbm, factors, sems.at[1])
    factor_copy.start()
    conf_copy.start()
    conf[TILES] = jnp.zeros((BS, BS), BF)
    live = count[0]

    for b in range(UB):
        heads[b] = 0

    def tally(t, carry):
        b = users[t]
        heads[b] = heads[b] + 1
        return carry

    lax.fori_loop(0, live, tally, 0)
    ends = []
    begin = jnp.int32(0)
    for b in range(UB):
        size = heads[b]
        heads[b] = begin
        begin = begin + (size + GROUP - 1) // GROUP * GROUP
        ends.append(begin)
    total = ends[-1]

    def blank(s, carry):
        slots[s] = TILES
        return carry

    lax.fori_loop(0, total, blank, 0)

    def place(t, carry):
        b = users[t]
        s = heads[b]
        slots[s] = t
        heads[b] = s + 1
        return carry

    lax.fori_loop(0, live, place, 0)

    factor_copy.wait()

    def gram_step(p, carry):
        pair = factors[pl.ds(pl.multiple_of(p * 2 * BS, 2 * BS), 2 * BS), :]
        weights = jnp.concatenate(
            [exposure[pl.ds(2 * p, 1), :], exposure[pl.ds(2 * p + 1, 1), :]], axis=1
        )
        scaled = pair.astype(F32).T * weights
        high = scaled.astype(BF)
        low = (scaled - high.astype(F32)).astype(BF)
        return carry + nn(high, pair) + nn(low, pair)

    gram[...] = jnp.zeros_like(gram)

    def gram_four(p, carry):
        sub = gram_step(2 * p, 0.0) + gram_step(2 * p + 1, 0.0)
        gram[...] += sub
        return carry

    lax.fori_loop(0, TILES // 4, gram_four, 0)
    conf_copy.wait()

    def group_of(g):
        first = g * GROUP
        b = (
            (first >= ends[0]).astype(jnp.int32)
            + (first >= ends[1]).astype(jnp.int32)
            + (first >= ends[2]).astype(jnp.int32)
        )
        confs, parts, levels = [], [], []
        for j in range(GROUP):
            t = slots[first + j]
            item = items[jnp.minimum(t, TILES - 1)]
            confs.append(conf[t])
            parts.append(factors[pl.ds(pl.multiple_of(item * BS, BS), BS), :])
            levels.append(exposure[pl.ds(item, 1), :])
        rows = pl.ds(pl.multiple_of(b * BS, BS), BS)
        return rows, jnp.concatenate(confs, axis=1), jnp.concatenate(parts, axis=0), levels

    right[...] = jnp.zeros_like(right)

    def right_step(g, carry):
        rows, weights, parts, _ = group_of(g)
        right[rows, :] += nn(weights, parts)
        return carry

    groups = total // GROUP
    lax.fori_loop(0, groups, right_step, 0)

    def map_step(g, carry):
        rows, weights, parts, levels = group_of(g)
        wide = weights.astype(F32)
        excess = jnp.where(wide > 0, wide - jnp.concatenate(levels, axis=1), 0.0)
        scores = nt(narrow[rows, :], parts)
        mapped[rows, :] += nn((excess * scores).astype(BF), parts)
        return carry

    residual[...] = right[...]
    direction[...] = right[...]
    answer[...] = jnp.zeros_like(answer)
    norm = row_sum(right[...] * right[...])
    for step in range(STEPS):
        way = direction[...]
        narrow[...] = way.astype(BF)
        mapped[...] = way + jnp.dot(way, gram[...], precision=HIGH, preferred_element_type=F32)
        lax.fori_loop(0, groups, map_step, 0)
        image = mapped[...]
        stride = norm / row_sum(way * image)
        answer[...] += stride * way
        if step < STEPS - 1:
            rest = residual[...] - stride * image
            residual[...] = rest
            norm_next = row_sum(rest * rest)
            direction[...] = rest + norm_next / norm * way
            norm = norm_next

    result = answer[...].astype(BF)
    out[...] = result

    def send_row(t, carry):
        rows = pl.ds(pl.multiple_of(users[t] * BS, BS), BS)
        pltpu.make_async_copy(out.at[rows, :], rows_hbm.at[items[t]], sems.at[2]).start()
        return carry

    lax.fori_loop(0, TILES, send_row, 0)
    gram_out[...] = tn(result, result)
    pltpu.make_async_copy(rows_hbm, rows_hbm, sems.at[2]).wait()


def user_half(items, users, count, conf, factors, exposure):
    smem = pl.BlockSpec(memory_space=pltpu.SMEM)
    vmem = pl.BlockSpec(memory_space=pltpu.VMEM)
    far = pl.BlockSpec(memory_space=pl.ANY)
    wide = pltpu.VMEM((UB * BS, RANK), F32)
    return pl.pallas_call(
        user_kernel,
        out_shape=(
            jax.ShapeDtypeStruct((UB * BS, RANK), BF),
            jax.ShapeDtypeStruct((TILES, BS, RANK), BF),
            jax.ShapeDtypeStruct((RANK, RANK), F32),
        ),
        in_specs=[smem, smem, smem, far, far, vmem],
        out_specs=(vmem, far, vmem),
        scratch_shapes=[
            pltpu.VMEM((TILES + 1, BS, BS), BF),
            pltpu.VMEM((TILES * BS, RANK), BF),
            pltpu.SMEM((SLOTS,), jnp.int32),
            pltpu.SMEM((UB,), jnp.int32),
            pltpu.VMEM((RANK, RANK), F32),
            wide,
            wide,
            pltpu.VMEM((UB * BS, RANK), BF),
            wide,
            wide,
            wide,
            pltpu.SemaphoreType.DMA((3,)),
        ],
        compiler_params=pltpu.CompilerParams(vmem_limit_bytes=VMEM_BYTES),
        name="user_half",
    )(items, users, count, conf, factors, exposure)


ITEM_GROUP = 8


def item_kernel(
    conf_hbm, rows_hbm, exposure, user_gram,
    out,
    conf, rows, mapped, narrow, sems,
):
    chunk = ITEM_GROUP
    chunks = TILES // chunk
    copies = []
    for c in range(chunks):
        part = pl.ds(c * chunk, chunk)
        copies.append(
            (
                pltpu.make_async_copy(rows_hbm.at[part], rows.at[part], sems.at[0, c]),
                pltpu.make_async_copy(conf_hbm.at[part], conf.at[part], sems.at[1, c]),
            )
        )
    for pair in copies:
        pair[0].start()
        pair[1].start()
    level = jnp.broadcast_to(exposure[...], (BS, BS)).T
    level_wide = jnp.concatenate([level] * chunk, axis=1)
    level_rank = jnp.concatenate([level] * (RANK // BS), axis=1)

    def chunk_of(c):
        weights = jnp.concatenate([conf[c * chunk + j] for j in range(chunk)], axis=1)
        part = rows[pl.ds(c * chunk, chunk)].reshape(chunk * BS, RANK)
        return weights, part

    mapped[...] = jnp.zeros_like(mapped)
    for c in range(chunks):
        copies[c][0].wait()
        copies[c][1].wait()
        weights, part = chunk_of(c)
        mapped[...] += nn(weights, part)
    right = mapped[...]

    def map_step(c, carry):
        weights, part = chunk_of(c)
        wide = weights.astype(F32)
        excess = jnp.where(wide > 0, wide - level_wide, 0.0)
        scores = nt(narrow[...], part)
        mapped[...] += nn((excess * scores).astype(BF), part)
        return carry

    residual = right
    way = right
    answer = jnp.zeros_like(right)
    norm = row_sum(right * right)
    for step in range(STEPS):
        narrow[...] = way.astype(BF)
        term = jnp.dot(way, user_gram[...], precision=HIGH, preferred_element_type=F32)
        mapped[...] = way + level_rank * term
        lax.fori_loop(0, chunks, map_step, 0)
        image = mapped[...]
        stride = norm / row_sum(way * image)
        answer = answer + stride * way
        if step < STEPS - 1:
            residual = residual - stride * image
            norm_next = row_sum(residual * residual)
            way = residual + norm_next / norm * way
            norm = norm_next
    out[...] = (answer * (float(TILES) ** 0.5)).astype(BF)


def item_half(conf, rows, exposure, user_gram):
    vmem = pl.BlockSpec(memory_space=pltpu.VMEM)
    far = pl.BlockSpec(memory_space=pl.ANY)
    return pl.pallas_call(
        item_kernel,
        out_shape=jax.ShapeDtypeStruct((BS, RANK), BF),
        in_specs=[far, far, vmem, vmem],
        out_specs=vmem,
        scratch_shapes=[
            pltpu.VMEM((TILES, BS, BS), BF),
            pltpu.VMEM((TILES, BS, RANK), BF),
            pltpu.VMEM((BS, RANK), F32),
            pltpu.VMEM((BS, RANK), BF),
            pltpu.SemaphoreType.DMA((2, TILES // ITEM_GROUP)),
        ],
        compiler_params=pltpu.CompilerParams(vmem_limit_bytes=VMEM_BYTES),
        name="item_half",
    )(conf, rows, exposure, user_gram)


def exchange(values, axes):
    return lax.all_to_all(values, axes, split_axis=0, concat_axis=0, tiled=True)


def body(item_factors, exposure, confidence, tile_items, tile_users, tile_count):
    conf_tiles = confidence[0]
    items = tile_items[0]
    users = tile_users[0]
    panels = lax.axis_size("blk")
    size = item_factors.shape[0]
    extra = 16
    tail = jnp.pad(exposure.reshape(-1, RANK), ((0, extra - size // RANK), (0, 0)))
    packed = jnp.concatenate([item_factors, tail], axis=0)
    gathered = exchange(
        jnp.broadcast_to(packed[None], (panels, size + extra, RANK)).reshape(-1, RANK), "blk"
    ).reshape(panels, size + extra, RANK)
    factors = gathered[:, :size].reshape(panels * size, RANK)
    levels = gathered[:, size : size + size // RANK].reshape(TILES, BS).astype(F32)
    send_conf = send_conf_of(items, tile_count, conf_tiles)
    got_conf = exchange(send_conf, BOTH)
    user_factors, send_rows, local_gram = user_half(
        items, users, tile_count, conf_tiles, factors, levels
    )
    got_rows = exchange(send_rows, BOTH)
    pieces = exchange(local_gram.reshape(TILES, -1, RANK), BOTH)
    mine = jnp.sum(pieces, axis=0) * (1.0 / (UB * BS))
    user_gram = exchange(
        jnp.broadcast_to(mine[None], (TILES,) + mine.shape), BOTH
    ).reshape(RANK, RANK)
    own = lax.dynamic_slice_in_dim(exposure, lax.axis_index("grp") * BS, BS)
    item_update = item_half(got_conf, got_rows, own.astype(F32).reshape(1, BS), user_gram)
    return user_factors, item_update, user_gram


def solution(mesh):
    placed = (
        P("blk", None),
        P("blk"),
        P(BOTH, None, None, None),
        P(BOTH, None),
        P(BOTH, None),
        P(BOTH),
    )
    return jax.shard_map(
        body,
        mesh=mesh,
        in_specs=placed,
        out_specs=(P(BOTH, None), P(BOTH, None), P()),
        check_vma=False,
    )
```

```python
import functools

import jax
import jax.numpy as jnp
from jax import lax
from jax.experimental import pallas as pl
from jax.experimental.pallas import tpu as pltpu
from jax.sharding import PartitionSpec as P

UB = 4
BS = 128
RANK = 256
TILES = 128
STEPS = 3
GROUP = 8
BATCH = 3
SLOTS = TILES + (UB + BATCH) * GROUP
HIGH = lax.Precision.HIGHEST
BF = jnp.bfloat16
F32 = jnp.float32
VMEM_BYTES = 56 * 1024 * 1024
BOTH = ("blk", "grp")
SIDE = 4
XLO = 2
CORES = 2
HALF = 256
PART_A = 112
PART_B = HALF - PART_A
TAIL = 16
OFFSETS = (0, 1, -1, 2)


def place_of(x, y, z, core):
    panel = ((y % SIDE) * XLO + x % XLO) * SIDE + z % SIDE
    return panel * 4 + (x % SIDE) // XLO * CORES + core


def from_offset(dx=0, dy=0, dz=0, flip=0):
    return [
        (place_of(x + dx, y + dy, z + dz, core ^ flip), place_of(x, y, z, core))
        for x in range(SIDE)
        for y in range(SIDE)
        for z in range(SIDE)
        for core in range(CORES)
    ]


def fetch(values, **offset):
    return lax.ppermute(values, BOTH, from_offset(**offset))


def nt(a, b):
    return lax.dot_general(a, b, (((1,), (1,)), ((), ())), preferred_element_type=F32)


def nn(a, b):
    return lax.dot_general(a, b, (((1,), (0,)), ((), ())), preferred_element_type=F32)


def tn(a, b):
    return lax.dot_general(a, b, (((0,), (0,)), ((), ())), preferred_element_type=F32)


def row_sum(v):
    return jnp.sum(v, axis=1, keepdims=True)


def send_kernel(items, count, conf, out):
    def one(t, carry):
        tile = conf[t]
        tile = jnp.where(t < count[0], tile, jnp.zeros_like(tile))
        out[items[t]] = tile.T
        return carry

    lax.fori_loop(0, TILES, one, 0, unroll=4)


def send_conf_of(items, count, conf):
    smem = pl.BlockSpec(memory_space=pltpu.SMEM)
    vmem = pl.BlockSpec(memory_space=pltpu.VMEM)
    return pl.pallas_call(
        send_kernel,
        out_shape=jax.ShapeDtypeStruct((TILES, BS, BS), BF),
        in_specs=[smem, smem, vmem],
        out_specs=vmem,
        compiler_params=pltpu.CompilerParams(vmem_limit_bytes=VMEM_BYTES),
        cost_estimate=pl.CostEstimate(flops=0, bytes_accessed=16_000_000, transcendentals=0),
        name="send_conf",
    )(items, count, conf)


def user_kernel(
    items, users, count, gram_here, gram_there, conf_hbm, *rest,
):
    pieces, rest = rest[:16], rest[16:]
    (
        out, rows_hbm, gram_out,
        conf, factors, tails, exposure, slots, heads, gram, right, direction, narrow, mapped, answer, residual, sems,
    ) = rest
    conf_copy = pltpu.make_async_copy(conf_hbm, conf.at[pl.ds(0, TILES)], sems.at[0])
    panel = lax.axis_index("blk")
    core = lax.rem(lax.axis_index("grp"), CORES)
    here = (lax.div(panel, XLO * SIDE), lax.rem(lax.div(panel, SIDE), XLO), lax.rem(panel, SIDE))
    n = 0
    for kind in range(2):
        for flip in range(CORES):
            for outer in OFFSETS:
                for j, inner in enumerate(OFFSETS):
                    dy, dz = (inner, outer) if kind == 0 else (outer, inner)
                    y = lax.rem(here[0] + dy + SIDE, SIDE)
                    z = lax.rem(here[2] + dz + SIDE, SIDE)
                    for k in range(XLO):
                        x = here[1] if k == 0 else 1 - here[1]
                        half = ((y * XLO + x) * SIDE + z) * 2 + (core if flip == 0 else 1 - core)
                        source = pieces[n].at[j * XLO + k]
                        first = half * HALF + (0 if kind == 0 else PART_A)
                        size = PART_A if kind == 0 else PART_B
                        pltpu.make_async_copy(
                            source.at[pl.ds(0, size)],
                            factors.at[pl.ds(pl.multiple_of(first, 16), size)],
                            sems.at[1],
                        ).start()
                        if kind == 0:
                            pltpu.make_async_copy(
                                source.at[pl.ds(PART_A, TAIL)], tails.at[half], sems.at[3]
                            ).start()
                n += 1
    conf_copy.start()
    conf[TILES] = jnp.zeros((BS, BS), BF)
    live = count[0]

    for b in range(UB):
        heads[b] = 0

    def tally(t, carry):
        b = users[t]
        heads[b] = heads[b] + 1
        return carry

    lax.fori_loop(0, live, tally, 0)
    ends = []
    begin = jnp.int32(0)
    for b in range(UB):
        size = heads[b]
        heads[b] = begin
        begin = begin + (size + GROUP - 1) // GROUP * GROUP
        ends.append(begin)
    batches = (ends[-1] + GROUP * BATCH - 1) // (GROUP * BATCH)

    def blank(s, carry):
        slots[s] = TILES
        return carry

    lax.fori_loop(0, batches * (GROUP * BATCH), blank, 0)

    def place(t, carry):
        b = users[t]
        s = heads[b]
        slots[s] = t
        heads[b] = s + 1
        return carry

    lax.fori_loop(0, live, place, 0)

    pltpu.make_async_copy(factors, factors, sems.at[1]).wait()
    pltpu.make_async_copy(tails, tails, sems.at[3]).wait()

    def level_step(h, carry):
        row = tails[h].astype(F32)[0:1, :]
        exposure[pl.ds(2 * h, 1), :] = row[:, :BS]
        exposure[pl.ds(2 * h + 1, 1), :] = row[:, BS:]
        return carry

    lax.fori_loop(0, TILES // 2, level_step, 0, unroll=8)

    gram[...] = gram_here[...] + gram_there[...]
    conf_copy.wait()

    def group_of(g):
        first = g * GROUP
        b = (
            (first >= ends[0]).astype(jnp.int32)
            + (first >= ends[1]).astype(jnp.int32)
            + (first >= ends[2]).astype(jnp.int32)
        )
        confs, parts, levels = [], [], []
        for j in range(GROUP):
            t = slots[first + j]
            item = items[jnp.minimum(t, TILES - 1)]
            confs.append(conf[t])
            parts.append(factors[pl.ds(pl.multiple_of(item * BS, BS), BS), :])
            levels.append(exposure[pl.ds(item, 1), :])
        rows = pl.ds(pl.multiple_of(b * BS, BS), BS)
        return rows, jnp.concatenate(confs, axis=1), jnp.concatenate(parts, axis=0), levels

    right[...] = jnp.zeros_like(right)

    def right_step(g):
        rows, weights, parts, _ = group_of(g)
        right[rows, :] += nn(weights, parts)

    def each_group(step):
        def batch(n, carry):
            for j in range(BATCH):
                step(n * BATCH + j)
            return carry

        lax.fori_loop(0, batches, batch, 0)

    each_group(right_step)

    def map_step(g):
        rows, weights, parts, levels = group_of(g)
        wide = weights.astype(F32)
        excess = jnp.where(wide > 0, wide - jnp.concatenate(levels, axis=1), 0.0)
        scores = nt(narrow[rows, :], parts)
        mapped[rows, :] += nn((excess * scores).astype(BF), parts)

    residual[...] = right[...]
    direction[...] = right[...]
    answer[...] = jnp.zeros_like(answer)
    norm = row_sum(right[...] * right[...])
    for step in range(STEPS):
        way = direction[...]
        narrow[...] = way.astype(BF)
        mapped[...] = way + jnp.dot(way, gram[...], precision=HIGH, preferred_element_type=F32)
        each_group(map_step)
        image = mapped[...]
        stride = norm / row_sum(way * image)
        answer[...] += stride * way
        if step < STEPS - 1:
            rest = residual[...] - stride * image
            residual[...] = rest
            norm_next = row_sum(rest * rest)
            direction[...] = rest + norm_next / norm * way
            norm = norm_next

    result = answer[...].astype(BF)
    out[...] = result

    def send_row(t, carry):
        rows = pl.ds(pl.multiple_of(users[t] * BS, BS), BS)
        pltpu.make_async_copy(out.at[rows, :], rows_hbm.at[items[t]], sems.at[2]).start()
        return carry

    lax.fori_loop(0, TILES, send_row, 0)
    gram_out[...] = tn(result, result)
    pltpu.make_async_copy(rows_hbm, rows_hbm, sems.at[2]).wait()


def gram_kernel(*refs):
    parts_a, parts_b, out = refs[:SIDE], refs[SIDE : 2 * SIDE], refs[-1]
    out[...] = jnp.zeros_like(out)
    for n in range(SIDE):
        for m in range(SIDE):
            for k in range(XLO):
                first = parts_a[n][m * XLO + k]
                rows = jnp.concatenate([first[:PART_A], parts_b[m][n * XLO + k]], axis=0)
                weights = first[PART_A:].astype(F32)[0:1, :]
                scaled = rows.astype(F32).T * weights
                high = scaled.astype(BF)
                low = (scaled - high.astype(F32)).astype(BF)
                out[...] += nn(high, rows) + nn(low, rows)


def gram_half(parts_a, parts_b):
    vmem = pl.BlockSpec(memory_space=pltpu.VMEM)
    return pl.pallas_call(
        gram_kernel,
        out_shape=jax.ShapeDtypeStruct((RANK, RANK), F32),
        in_specs=[vmem] * (2 * SIDE),
        out_specs=vmem,
        compiler_params=pltpu.CompilerParams(vmem_limit_bytes=VMEM_BYTES),
        cost_estimate=pl.CostEstimate(flops=1_000_000_000, bytes_accessed=1_000_000, transcendentals=0),
        name="gram_half",
    )(*parts_a, *parts_b)


def user_half(items, users, count, grams, conf, pieces):
    smem = pl.BlockSpec(memory_space=pltpu.SMEM)
    vmem = pl.BlockSpec(memory_space=pltpu.VMEM)
    far = pl.BlockSpec(memory_space=pl.ANY)
    wide = pltpu.VMEM((UB * BS, RANK), F32)
    return pl.pallas_call(
        user_kernel,
        out_shape=(
            jax.ShapeDtypeStruct((UB * BS, RANK), BF),
            jax.ShapeDtypeStruct((TILES, BS, RANK), BF),
            jax.ShapeDtypeStruct((RANK, RANK), F32),
        ),
        in_specs=[smem, smem, smem, vmem, vmem, far] + [far] * len(pieces),
        out_specs=(vmem, far, vmem),
        scratch_shapes=[
            pltpu.VMEM((TILES + 1, BS, BS), BF),
            pltpu.VMEM((TILES * BS, RANK), BF),
            pltpu.VMEM((TILES // 2, TAIL, RANK), BF),
            pltpu.VMEM((TILES, BS), F32),
            pltpu.SMEM((SLOTS,), jnp.int32),
            pltpu.SMEM((UB,), jnp.int32),
            pltpu.VMEM((RANK, RANK), F32),
            wide,
            wide,
            pltpu.VMEM((UB * BS, RANK), BF),
            wide,
            wide,
            wide,
            pltpu.SemaphoreType.DMA((4,)),
        ],
        compiler_params=pltpu.CompilerParams(vmem_limit_bytes=VMEM_BYTES),
        cost_estimate=pl.CostEstimate(flops=5_000_000_000, bytes_accessed=4_000_000, transcendentals=0),
        name="user_half",
    )(items, users, count, *grams, conf, *pieces)


ITEM_GROUP = 16
CHUNKS = TILES // ITEM_GROUP


def item_tools(conf_hbm, rows_hbm, exposure, conf, rows, sems):
    def copies_of(c):
        part = pl.ds(c * ITEM_GROUP, ITEM_GROUP)
        return (
            pltpu.make_async_copy(rows_hbm.at[part], rows.at[part], sems.at[0, c]),
            pltpu.make_async_copy(conf_hbm.at[part], conf.at[part], sems.at[1, c]),
        )

    for c in range(CHUNKS):
        for copy in copies_of(c):
            copy.start()
    level = jnp.broadcast_to(exposure[...], (BS, BS)).T

    def chunk_of(c, waits):
        if waits:
            for copy in copies_of(c):
                copy.wait()
        weights = jnp.concatenate([conf[c * ITEM_GROUP + j] for j in range(ITEM_GROUP)], axis=1)
        part = rows[pl.ds(c * ITEM_GROUP, ITEM_GROUP)].reshape(ITEM_GROUP * BS, RANK)
        return weights, part

    def add_right(target):
        def step(c, carry):
            weights, part = chunk_of(c, True)
            target[...] += nn(weights, part)
            return carry

        lax.fori_loop(0, CHUNKS, step, 0, unroll=2)

    def add_returned(target, narrow, waits=False):
        level_wide = jnp.concatenate([level] * ITEM_GROUP, axis=1)

        def step(c, carry):
            weights, part = chunk_of(c, waits)
            wide = weights.astype(F32)
            excess = jnp.where(wide > 0, wide - level_wide, 0.0)
            scores = nt(narrow[...], part)
            target[...] += nn((excess * scores).astype(BF), part)
            return carry

        lax.fori_loop(0, CHUNKS, step, 0, unroll=2)

    return level, add_right, add_returned


def right_kernel(conf_hbm, rows_hbm, exposure, right, returned, conf, rows, narrow, sems):
    _, add_right, add_returned = item_tools(conf_hbm, rows_hbm, exposure, conf, rows, sems)
    right[...] = jnp.zeros_like(right)
    add_right(right)
    narrow[...] = right[...].astype(BF)
    returned[...] = jnp.zeros_like(returned)
    add_returned(returned, narrow)


def item_kernel(
    conf_hbm, rows_hbm, exposure, user_gram, right, returned, out, conf, rows, narrow, mapped, sems
):
    level, _, add_returned = item_tools(conf_hbm, rows_hbm, exposure, conf, rows, sems)
    level_rank = jnp.concatenate([level] * (RANK // BS), axis=1)
    residual = right[...]
    way = residual
    answer = jnp.zeros_like(residual)
    norm = row_sum(residual * residual)
    for step in range(STEPS):
        term = jnp.dot(way, user_gram[...], precision=HIGH, preferred_element_type=F32)
        mapped[...] = way + level_rank * term
        if step == 0:
            mapped[...] += returned[...]
        else:
            narrow[...] = way.astype(BF)
            add_returned(mapped, narrow, step == 1)
        image = mapped[...]
        stride = norm / row_sum(way * image)
        answer = answer + stride * way
        if step < STEPS - 1:
            residual = residual - stride * image
            norm_next = row_sum(residual * residual)
            way = residual + norm_next / norm * way
            norm = norm_next
    out[...] = (answer * (float(TILES) ** 0.5)).astype(BF)


def item_call(kernel, name, outs, scratch, conf, rows, *small):
    vmem = pl.BlockSpec(memory_space=pltpu.VMEM)
    far = pl.BlockSpec(memory_space=pl.ANY)
    return pl.pallas_call(
        kernel,
        out_shape=outs,
        in_specs=[far, far] + [vmem] * len(small),
        out_specs=[vmem] * len(outs),
        scratch_shapes=[
            pltpu.VMEM((TILES, BS, BS), BF),
            pltpu.VMEM((TILES, BS, RANK), BF),
            pltpu.VMEM((BS, RANK), BF),
            *scratch,
            pltpu.SemaphoreType.DMA((2, CHUNKS)),
        ],
        compiler_params=pltpu.CompilerParams(vmem_limit_bytes=VMEM_BYTES),
        cost_estimate=pl.CostEstimate(flops=12_000_000_000, bytes_accessed=13_000_000, transcendentals=0),
        name=name,
    )(conf, rows, *small)


def item_start(conf, rows, exposure):
    wide = jax.ShapeDtypeStruct((BS, RANK), F32)
    return item_call(right_kernel, "item_start", [wide, wide], [], conf, rows, exposure)


def item_half(conf, rows, exposure, user_gram, right, returned):
    out = jax.ShapeDtypeStruct((BS, RANK), BF)
    scratch = [pltpu.VMEM((BS, RANK), F32)]
    return item_call(
        item_kernel, "item_half", [out], scratch, conf, rows, exposure, user_gram, right, returned
    )[0]


def exchange(values, axes):
    return lax.all_to_all(values, axes, split_axis=0, concat_axis=0, tiled=True)


def sum_lines(values, core):
    rows = values.shape[0] // CORES
    first = values[:rows]
    second = values[rows:]
    half = jnp.where(core == 0, first, second) + fetch(jnp.where(core == 0, second, first), flip=1)
    return sum_axis(sum_axis(half, "dx"), "dy")


def sum_axis(half, axis):
    near, far, across = (fetch(half, **{axis: d}) for d in OFFSETS[1:])
    return (half + across) + (near + far)


def sum_rest(half, core):
    half = sum_axis(half, "dz")
    other = fetch(half, flip=1)
    return jnp.concatenate(
        [jnp.where(core == 0, half, other), jnp.where(core == 0, other, half)], axis=0
    )


def body(item_factors, exposure, confidence, tile_items, tile_users, tile_count):
    conf_tiles = confidence[0]
    items = tile_items[0]
    users = tile_users[0]
    core = lax.rem(lax.axis_index("grp"), CORES)
    mine = lax.dynamic_slice_in_dim(item_factors, core * HALF, HALF)
    tail = jnp.pad(
        lax.dynamic_slice_in_dim(exposure, core * HALF, HALF)[None], ((0, TAIL - 1), (0, 0))
    )
    part_a = jnp.concatenate([mine[:PART_A], tail], axis=0)
    part_b = mine[PART_A:]
    part_a = jnp.stack([part_a, fetch(part_a, dx=1)])
    part_b = jnp.stack([part_b, fetch(part_b, dx=-1)])
    line_a = jnp.concatenate([part_a] + [fetch(part_a, dy=d) for d in OFFSETS[1:]], axis=0)
    line_b = jnp.concatenate([part_b] + [fetch(part_b, dz=d) for d in OFFSETS[1:]], axis=0)
    send_conf = send_conf_of(items, tile_count, conf_tiles)
    full_a = [line_a] + [fetch(line_a, dz=d) for d in OFFSETS[1:]]
    full_b = [line_b] + [fetch(line_b, dy=d) for d in OFFSETS[1:]]
    full_a[1:], full_b[1:], send_conf = lax.optimization_barrier(
        (full_a[1:], full_b[1:], send_conf)
    )
    got_conf = exchange(send_conf, BOTH)
    pieces = (
        full_a + [fetch(v, flip=1) for v in full_a]
        + full_b + [fetch(v, flip=1) for v in full_b]
    )
    gram_own = gram_half(full_a, full_b)
    user_factors, send_rows, local_gram = user_half(
        items, users, tile_count, (gram_own, fetch(gram_own, flip=1)), conf_tiles, pieces
    )
    got_rows = exchange(send_rows, BOTH)
    half_gram = sum_lines(local_gram, core)
    own = lax.dynamic_slice_in_dim(exposure, lax.axis_index("grp") * BS, BS)
    own = own.astype(F32).reshape(1, BS)
    right, returned = item_start(got_conf, got_rows, own)
    half_gram, right, returned = lax.optimization_barrier((half_gram, right, returned))
    user_gram = sum_rest(half_gram, core) * (1.0 / (UB * BS))
    item_update = item_half(got_conf, got_rows, own, user_gram, right, returned)
    return user_factors, item_update, user_gram


def solution(mesh):
    placed = (
        P("blk", None),
        P("blk"),
        P(BOTH, None, None, None),
        P(BOTH, None),
        P(BOTH, None),
        P(BOTH),
    )
    return jax.shard_map(
        body,
        mesh=mesh,
        in_specs=placed,
        out_specs=(P(BOTH, None), P(BOTH, None), P()),
        check_vma=False,
    )
```

```python
import functools

import jax
import jax.numpy as jnp
from jax import lax
from jax.experimental import pallas as pl
from jax.experimental.pallas import tpu as pltpu
from jax.sharding import PartitionSpec as P

UB = 4
BS = 128
RANK = 256
TILES = 128
STEPS = 3
GROUP = 8
BATCH = 3
SLOTS = TILES + (UB + BATCH) * GROUP
HIGH = lax.Precision.HIGHEST
BF = jnp.bfloat16
F32 = jnp.float32
VMEM_BYTES = 56 * 1024 * 1024
BOTH = ("blk", "grp")
SIDE = 4
XLO = 2
CORES = 2
HALF = 256
PART_A = 112
PART_B = HALF - PART_A
TAIL = 16
OFFSETS = (0, 1, -1, 2)


def place_of(x, y, z, core):
    panel = ((y % SIDE) * XLO + x % XLO) * SIDE + z % SIDE
    return panel * 4 + (x % SIDE) // XLO * CORES + core


def from_offset(dx=0, dy=0, dz=0, flip=0):
    return [
        (place_of(x + dx, y + dy, z + dz, core ^ flip), place_of(x, y, z, core))
        for x in range(SIDE)
        for y in range(SIDE)
        for z in range(SIDE)
        for core in range(CORES)
    ]


def fetch(values, **offset):
    return lax.ppermute(values, BOTH, from_offset(**offset))


def nt(a, b):
    return lax.dot_general(a, b, (((1,), (1,)), ((), ())), preferred_element_type=F32)


def nn(a, b):
    return lax.dot_general(a, b, (((1,), (0,)), ((), ())), preferred_element_type=F32)


def tn(a, b):
    return lax.dot_general(a, b, (((0,), (0,)), ((), ())), preferred_element_type=F32)


def row_sum(v):
    return jnp.sum(v, axis=1, keepdims=True)


def send_kernel(items, count, conf, out):
    def one(t, carry):
        tile = conf[t]
        tile = jnp.where(t < count[0], tile, jnp.zeros_like(tile))
        out[items[t]] = tile.T
        return carry

    lax.fori_loop(0, TILES, one, 0, unroll=4)


def send_conf_of(items, count, conf):
    smem = pl.BlockSpec(memory_space=pltpu.SMEM)
    vmem = pl.BlockSpec(memory_space=pltpu.VMEM)
    return pl.pallas_call(
        send_kernel,
        out_shape=jax.ShapeDtypeStruct((TILES, BS, BS), BF),
        in_specs=[smem, smem, vmem],
        out_specs=vmem,
        compiler_params=pltpu.CompilerParams(vmem_limit_bytes=VMEM_BYTES),
        cost_estimate=pl.CostEstimate(flops=0, bytes_accessed=16_000_000, transcendentals=0),
        name="send_conf",
    )(items, count, conf)


def user_kernel(
    items, users, count, gram_here, gram_there, conf_hbm, *rest,
):
    pieces, rest = rest[:16], rest[16:]
    (
        out, rows_hbm, gram_out,
        conf, factors, tails, exposure, slots, heads, gram, right, direction, narrow, mapped, answer, residual, sems,
    ) = rest
    conf_copy = pltpu.make_async_copy(conf_hbm, conf.at[pl.ds(0, TILES)], sems.at[0])
    panel = lax.axis_index("blk")
    core = lax.rem(lax.axis_index("grp"), CORES)
    here = (lax.div(panel, XLO * SIDE), lax.rem(lax.div(panel, SIDE), XLO), lax.rem(panel, SIDE))
    n = 0
    for kind in range(2):
        for flip in range(CORES):
            for outer in OFFSETS:
                for j, inner in enumerate(OFFSETS):
                    dy, dz = (inner, outer) if kind == 0 else (outer, inner)
                    y = lax.rem(here[0] + dy + SIDE, SIDE)
                    z = lax.rem(here[2] + dz + SIDE, SIDE)
                    for k in range(XLO):
                        x = here[1] if k == 0 else 1 - here[1]
                        half = ((y * XLO + x) * SIDE + z) * 2 + (core if flip == 0 else 1 - core)
                        source = pieces[n].at[j * XLO + k]
                        first = half * HALF + (0 if kind == 0 else PART_A)
                        size = PART_A if kind == 0 else PART_B
                        pltpu.make_async_copy(
                            source.at[pl.ds(0, size)],
                            factors.at[pl.ds(pl.multiple_of(first, 16), size)],
                            sems.at[1],
                        ).start()
                        if kind == 0:
                            pltpu.make_async_copy(
                                source.at[pl.ds(PART_A, TAIL)], tails.at[half], sems.at[3]
                            ).start()
                n += 1
    conf_copy.start()
    conf[TILES] = jnp.zeros((BS, BS), BF)
    live = count[0]

    for b in range(UB):
        heads[b] = 0

    def tally(t, carry):
        b = users[t]
        heads[b] = heads[b] + 1
        return carry

    lax.fori_loop(0, live, tally, 0)
    ends = []
    begin = jnp.int32(0)
    for b in range(UB):
        size = heads[b]
        heads[b] = begin
        begin = begin + (size + GROUP - 1) // GROUP * GROUP
        ends.append(begin)
    batches = (ends[-1] + GROUP * BATCH - 1) // (GROUP * BATCH)

    def blank(s, carry):
        slots[s] = TILES
        return carry

    lax.fori_loop(0, batches * (GROUP * BATCH), blank, 0)

    def place(t, carry):
        b = users[t]
        s = heads[b]
        slots[s] = t
        heads[b] = s + 1
        return carry

    lax.fori_loop(0, live, place, 0)

    pltpu.make_async_copy(factors, factors, sems.at[1]).wait()
    pltpu.make_async_copy(tails, tails, sems.at[3]).wait()

    def level_step(h, carry):
        row = tails[h].astype(F32)[0:1, :]
        exposure[pl.ds(2 * h, 1), :] = row[:, :BS]
        exposure[pl.ds(2 * h + 1, 1), :] = row[:, BS:]
        return carry

    lax.fori_loop(0, TILES // 2, level_step, 0, unroll=8)

    gram[...] = gram_here[...] + gram_there[...]
    conf_copy.wait()

    def group_of(g):
        first = g * GROUP
        b = (
            (first >= ends[0]).astype(jnp.int32)
            + (first >= ends[1]).astype(jnp.int32)
            + (first >= ends[2]).astype(jnp.int32)
        )
        confs, parts, levels = [], [], []
        for j in range(GROUP):
            t = slots[first + j]
            item = items[jnp.minimum(t, TILES - 1)]
            confs.append(conf[t])
            parts.append(factors[pl.ds(pl.multiple_of(item * BS, BS), BS), :])
            levels.append(exposure[pl.ds(item, 1), :])
        rows = pl.ds(pl.multiple_of(b * BS, BS), BS)
        return rows, jnp.concatenate(confs, axis=1), jnp.concatenate(parts, axis=0), levels

    right[...] = jnp.zeros_like(right)

    def right_step(g):
        rows, weights, parts, _ = group_of(g)
        right[rows, :] += nn(weights, parts)

    def each_group(step):
        def batch(n, carry):
            for j in range(BATCH):
                step(n * BATCH + j)
            return carry

        lax.fori_loop(0, batches, batch, 0)

    each_group(right_step)

    def map_step(g):
        rows, weights, parts, levels = group_of(g)
        wide = weights.astype(F32)
        excess = jnp.where(wide > 0, wide - jnp.concatenate(levels, axis=1), 0.0)
        scores = nt(narrow[rows, :], parts)
        mapped[rows, :] += nn((excess * scores).astype(BF), parts)

    residual[...] = right[...]
    direction[...] = right[...]
    answer[...] = jnp.zeros_like(answer)
    norm = row_sum(right[...] * right[...])
    for step in range(STEPS):
        way = direction[...]
        narrow[...] = way.astype(BF)
        mapped[...] = way + jnp.dot(way, gram[...], precision=HIGH, preferred_element_type=F32)
        each_group(map_step)
        image = mapped[...]
        stride = norm / row_sum(way * image)
        answer[...] += stride * way
        if step < STEPS - 1:
            rest = residual[...] - stride * image
            residual[...] = rest
            norm_next = row_sum(rest * rest)
            direction[...] = rest + norm_next / norm * way
            norm = norm_next

    result = answer[...].astype(BF)
    out[...] = result

    def send_row(t, carry):
        rows = pl.ds(pl.multiple_of(users[t] * BS, BS), BS)
        pltpu.make_async_copy(out.at[rows, :], rows_hbm.at[items[t]], sems.at[2]).start()
        return carry

    lax.fori_loop(0, TILES, send_row, 0)
    gram_out[...] = tn(result, result)
    pltpu.make_async_copy(rows_hbm, rows_hbm, sems.at[2]).wait()


def gram_kernel(*refs):
    parts_a, parts_b, out = refs[:SIDE], refs[SIDE : 2 * SIDE], refs[-1]
    out[...] = jnp.zeros_like(out)
    for n in range(SIDE):
        for m in range(SIDE):
            for k in range(XLO):
                first = parts_a[n][m * XLO + k]
                rows = jnp.concatenate([first[:PART_A], parts_b[m][n * XLO + k]], axis=0)
                weights = first[PART_A:].astype(F32)[0:1, :]
                scaled = rows.astype(F32).T * weights
                high = scaled.astype(BF)
                low = (scaled - high.astype(F32)).astype(BF)
                out[...] += nn(high, rows) + nn(low, rows)


def gram_half(parts_a, parts_b):
    vmem = pl.BlockSpec(memory_space=pltpu.VMEM)
    return pl.pallas_call(
        gram_kernel,
        out_shape=jax.ShapeDtypeStruct((RANK, RANK), F32),
        in_specs=[vmem] * (2 * SIDE),
        out_specs=vmem,
        compiler_params=pltpu.CompilerParams(vmem_limit_bytes=VMEM_BYTES),
        cost_estimate=pl.CostEstimate(flops=1_000_000_000, bytes_accessed=1_000_000, transcendentals=0),
        name="gram_half",
    )(*parts_a, *parts_b)


def user_half(items, users, count, grams, conf, pieces):
    smem = pl.BlockSpec(memory_space=pltpu.SMEM)
    vmem = pl.BlockSpec(memory_space=pltpu.VMEM)
    far = pl.BlockSpec(memory_space=pl.ANY)
    wide = pltpu.VMEM((UB * BS, RANK), F32)
    return pl.pallas_call(
        user_kernel,
        out_shape=(
            jax.ShapeDtypeStruct((UB * BS, RANK), BF),
            jax.ShapeDtypeStruct((TILES, BS, RANK), BF),
            jax.ShapeDtypeStruct((RANK, RANK), F32),
        ),
        in_specs=[smem, smem, smem, vmem, vmem, far] + [far] * len(pieces),
        out_specs=(vmem, far, vmem),
        scratch_shapes=[
            pltpu.VMEM((TILES + 1, BS, BS), BF),
            pltpu.VMEM((TILES * BS, RANK), BF),
            pltpu.VMEM((TILES // 2, TAIL, RANK), BF),
            pltpu.VMEM((TILES, BS), F32),
            pltpu.SMEM((SLOTS,), jnp.int32),
            pltpu.SMEM((UB,), jnp.int32),
            pltpu.VMEM((RANK, RANK), F32),
            wide,
            wide,
            pltpu.VMEM((UB * BS, RANK), BF),
            wide,
            wide,
            wide,
            pltpu.SemaphoreType.DMA((4,)),
        ],
        compiler_params=pltpu.CompilerParams(vmem_limit_bytes=VMEM_BYTES),
        cost_estimate=pl.CostEstimate(flops=5_000_000_000, bytes_accessed=4_000_000, transcendentals=0),
        name="user_half",
    )(items, users, count, *grams, conf, *pieces)


ITEM_GROUP = 16
CHUNKS = TILES // ITEM_GROUP


def item_tools(conf_hbm, rows_hbm, exposure, conf, rows, sems):
    def copies_of(c):
        part = pl.ds(c * ITEM_GROUP, ITEM_GROUP)
        return (
            pltpu.make_async_copy(rows_hbm.at[part], rows.at[part], sems.at[0, c]),
            pltpu.make_async_copy(conf_hbm.at[part], conf.at[part], sems.at[1, c]),
        )

    for c in range(CHUNKS):
        for copy in copies_of(c):
            copy.start()
    level = jnp.broadcast_to(exposure[...], (BS, BS)).T

    def chunk_of(c, waits):
        if waits:
            for copy in copies_of(c):
                copy.wait()
        weights = jnp.concatenate([conf[c * ITEM_GROUP + j] for j in range(ITEM_GROUP)], axis=1)
        part = rows[pl.ds(c * ITEM_GROUP, ITEM_GROUP)].reshape(ITEM_GROUP * BS, RANK)
        return weights, part

    def add_right(target):
        def step(c, carry):
            weights, part = chunk_of(c, True)
            target[...] += nn(weights, part)
            return carry

        lax.fori_loop(0, CHUNKS, step, 0, unroll=4)

    def add_returned(target, narrow, waits=False):
        level_wide = jnp.concatenate([level] * ITEM_GROUP, axis=1)

        def step(c, carry):
            weights, part = chunk_of(c, waits)
            wide = weights.astype(F32)
            excess = jnp.where(wide > 0, wide - level_wide, 0.0)
            scores = nt(narrow[...], part)
            target[...] += nn((excess * scores).astype(BF), part)
            return carry

        lax.fori_loop(0, CHUNKS, step, 0, unroll=4)

    return level, add_right, add_returned


def right_kernel(conf_hbm, rows_hbm, exposure, right, returned, conf, rows, narrow, sems):
    _, add_right, add_returned = item_tools(conf_hbm, rows_hbm, exposure, conf, rows, sems)
    right[...] = jnp.zeros_like(right)
    add_right(right)
    narrow[...] = right[...].astype(BF)
    returned[...] = jnp.zeros_like(returned)
    add_returned(returned, narrow)


def item_kernel(
    conf_hbm, rows_hbm, exposure, user_gram, right, returned, out, conf, rows, narrow, mapped, sems
):
    level, _, add_returned = item_tools(conf_hbm, rows_hbm, exposure, conf, rows, sems)
    level_rank = jnp.concatenate([level] * (RANK // BS), axis=1)
    residual = right[...]
    way = residual
    answer = jnp.zeros_like(residual)
    norm = row_sum(residual * residual)
    for step in range(STEPS):
        term = jnp.dot(way, user_gram[...], precision=HIGH, preferred_element_type=F32)
        mapped[...] = way + level_rank * term
        if step == 0:
            mapped[...] += returned[...]
        else:
            narrow[...] = way.astype(BF)
            add_returned(mapped, narrow, step == 1)
        image = mapped[...]
        stride = norm / row_sum(way * image)
        answer = answer + stride * way
        if step < STEPS - 1:
            residual = residual - stride * image
            norm_next = row_sum(residual * residual)
            way = residual + norm_next / norm * way
            norm = norm_next
    out[...] = (answer * (float(TILES) ** 0.5)).astype(BF)


def item_call(kernel, name, outs, scratch, conf, rows, *small):
    vmem = pl.BlockSpec(memory_space=pltpu.VMEM)
    far = pl.BlockSpec(memory_space=pl.ANY)
    return pl.pallas_call(
        kernel,
        out_shape=outs,
        in_specs=[far, far] + [vmem] * len(small),
        out_specs=[vmem] * len(outs),
        scratch_shapes=[
            pltpu.VMEM((TILES, BS, BS), BF),
            pltpu.VMEM((TILES, BS, RANK), BF),
            pltpu.VMEM((BS, RANK), BF),
            *scratch,
            pltpu.SemaphoreType.DMA((2, CHUNKS)),
        ],
        compiler_params=pltpu.CompilerParams(vmem_limit_bytes=VMEM_BYTES),
        cost_estimate=pl.CostEstimate(flops=12_000_000_000, bytes_accessed=13_000_000, transcendentals=0),
        name=name,
    )(conf, rows, *small)


def item_start(conf, rows, exposure):
    wide = jax.ShapeDtypeStruct((BS, RANK), F32)
    return item_call(right_kernel, "item_start", [wide, wide], [], conf, rows, exposure)


def item_half(conf, rows, exposure, user_gram, right, returned):
    out = jax.ShapeDtypeStruct((BS, RANK), BF)
    scratch = [pltpu.VMEM((BS, RANK), F32)]
    return item_call(
        item_kernel, "item_half", [out], scratch, conf, rows, exposure, user_gram, right, returned
    )[0]


def exchange(values, axes):
    return lax.all_to_all(values, axes, split_axis=0, concat_axis=0, tiled=True)


def sum_lines(values, core):
    rows = values.shape[0] // CORES
    first = values[:rows]
    second = values[rows:]
    half = jnp.where(core == 0, first, second) + fetch(jnp.where(core == 0, second, first), flip=1)
    return sum_axis(half, "dx")


def sum_axis(half, axis):
    near, far, across = (fetch(half, **{axis: d}) for d in OFFSETS[1:])
    return (half + across) + (near + far)


def sum_rest(half, core):
    half = sum_axis(half, "dz")
    other = fetch(half, flip=1)
    return jnp.concatenate(
        [jnp.where(core == 0, half, other), jnp.where(core == 0, other, half)], axis=0
    )


def body(item_factors, exposure, confidence, tile_items, tile_users, tile_count):
    conf_tiles = confidence[0]
    items = tile_items[0]
    users = tile_users[0]
    core = lax.rem(lax.axis_index("grp"), CORES)
    mine = lax.dynamic_slice_in_dim(item_factors, core * HALF, HALF)
    tail = jnp.pad(
        lax.dynamic_slice_in_dim(exposure, core * HALF, HALF)[None], ((0, TAIL - 1), (0, 0))
    )
    part_a = jnp.concatenate([mine[:PART_A], tail], axis=0)
    part_b = mine[PART_A:]
    part_a = jnp.stack([part_a, fetch(part_a, dx=1)])
    part_b = jnp.stack([part_b, fetch(part_b, dx=-1)])
    line_a = jnp.concatenate([part_a] + [fetch(part_a, dy=d) for d in OFFSETS[1:]], axis=0)
    line_b = jnp.concatenate([part_b] + [fetch(part_b, dz=d) for d in OFFSETS[1:]], axis=0)
    send_conf = send_conf_of(items, tile_count, conf_tiles)
    line_a, line_b = lax.optimization_barrier((line_a, line_b))
    full_a = [line_a] + [fetch(line_a, dz=d) for d in OFFSETS[1:]]
    full_b = [line_b] + [fetch(line_b, dy=d) for d in OFFSETS[1:]]
    full_a[1:], full_b[1:], send_conf = lax.optimization_barrier(
        (full_a[1:], full_b[1:], send_conf)
    )
    got_conf = exchange(send_conf, BOTH)
    pieces = (
        full_a + [fetch(v, flip=1) for v in full_a]
        + full_b + [fetch(v, flip=1) for v in full_b]
    )
    gram_own = gram_half(full_a, full_b)
    user_factors, send_rows, local_gram = user_half(
        items, users, tile_count, (gram_own, fetch(gram_own, flip=1)), conf_tiles, pieces
    )
    got_rows = exchange(send_rows, BOTH)
    half_gram = sum_lines(local_gram, core)
    own = lax.dynamic_slice_in_dim(exposure, lax.axis_index("grp") * BS, BS)
    own = own.astype(F32).reshape(1, BS)
    half_gram, got_rows, got_conf = lax.optimization_barrier((half_gram, got_rows, got_conf))
    right, returned = item_start(got_conf, got_rows, own)
    half_gram = sum_axis(half_gram, "dy")
    half_gram, right, returned = lax.optimization_barrier((half_gram, right, returned))
    user_gram = sum_rest(half_gram, core) * (1.0 / (UB * BS))
    item_update = item_half(got_conf, got_rows, own, user_gram, right, returned)
    return user_factors, item_update, user_gram


def solution(mesh):
    placed = (
        P("blk", None),
        P("blk"),
        P(BOTH, None, None, None),
        P(BOTH, None),
        P(BOTH, None),
        P(BOTH),
    )
    return jax.shard_map(
        body,
        mesh=mesh,
        in_specs=placed,
        out_specs=(P(BOTH, None), P(BOTH, None), P()),
        check_vma=False,
    )
```

```python
import functools

import jax
import jax.numpy as jnp
from jax import lax
from jax.experimental import pallas as pl
from jax.experimental.pallas import tpu as pltpu
from jax.sharding import PartitionSpec as P

UB = 4
BS = 128
RANK = 256
TILES = 128
STEPS = 3
GROUP = 8
BATCH = 3
SLOTS = TILES + (UB + BATCH) * GROUP
HIGH = lax.Precision.HIGHEST
BF = jnp.bfloat16
F32 = jnp.float32
VMEM_BYTES = 56 * 1024 * 1024
BOTH = ("blk", "grp")
SIDE = 4
XLO = 2
CORES = 2
HALF = 256
PART_A = 112
PART_B = HALF - PART_A
TAIL = 16
OFFSETS = (0, 1, -1, 2)
ROWS = (48, 48, 32)
STARTS = (0, 48, 96)
ORDERS = (("dx", "dy", "dz"), ("dy", "dz", "dx"), ("dz", "dx", "dy"))
MESSAGES = len(OFFSETS) * CORES


def place_of(x, y, z, core):
    panel = ((y % SIDE) * XLO + x % XLO) * SIDE + z % SIDE
    return panel * 4 + (x % SIDE) // XLO * CORES + core


def from_offset(dx=0, dy=0, dz=0, flip=0):
    return [
        (place_of(x + dx, y + dy, z + dz, core ^ flip), place_of(x, y, z, core))
        for x in range(SIDE)
        for y in range(SIDE)
        for z in range(SIDE)
        for core in range(CORES)
    ]


def fetch(values, **offset):
    return lax.ppermute(values, BOTH, from_offset(**offset))


def nt(a, b):
    return lax.dot_general(a, b, (((1,), (1,)), ((), ())), preferred_element_type=F32)


def nn(a, b):
    return lax.dot_general(a, b, (((1,), (0,)), ((), ())), preferred_element_type=F32)


def tn(a, b):
    return lax.dot_general(a, b, (((0,), (0,)), ((), ())), preferred_element_type=F32)


def row_sum(v):
    return jnp.sum(v, axis=1, keepdims=True)


def coordinates():
    panel = lax.axis_index("blk")
    group = lax.axis_index("grp")
    return split_place(panel * 4 + group)


def split_place(place):
    x = (place >> 1 & 1) * 2 + (place >> 4 & 1)
    return {"dx": x, "dy": place >> 5, "dz": place >> 2 & 3}, place & 1


def join_place(at, core):
    x, y, z = at["dx"], at["dy"], at["dz"]
    return y * 32 + (x & 1) * 16 + z * 4 + (x >> 1) * 2 + core


def offset_index(there, here):
    step = (there - here) & 3
    return step ^ (step >> 1)


def send_kernel(items, count, conf, out):
    def one(t, carry):
        tile = conf[t]
        tile = jnp.where(t < count[0], tile, jnp.zeros_like(tile))
        out[items[t]] = tile.T
        return carry

    lax.fori_loop(0, TILES, one, 0, unroll=4)


def send_conf_of(items, count, conf):
    smem = pl.BlockSpec(memory_space=pltpu.SMEM)
    vmem = pl.BlockSpec(memory_space=pltpu.VMEM)
    return pl.pallas_call(
        send_kernel,
        out_shape=jax.ShapeDtypeStruct((TILES, BS, BS), BF),
        in_specs=[smem, smem, vmem],
        out_specs=vmem,
        compiler_params=pltpu.CompilerParams(vmem_limit_bytes=VMEM_BYTES),
        cost_estimate=pl.CostEstimate(flops=0, bytes_accessed=16_000_000, transcendentals=0),
        name="send_conf",
    )(items, count, conf)


def user_kernel(
    items, users, count, gram_here, gram_there, tail_ref, conf_hbm, *rest,
):
    pieces, rest = rest[:16], rest[16:]
    (
        out, send_0, send_1, send_2, gram_out,
        conf, factors, tails, exposure, slots, heads, gram, right, direction, narrow, mapped, answer, residual, sems,
    ) = rest
    conf_copy = pltpu.make_async_copy(conf_hbm, conf.at[pl.ds(0, TILES)], sems.at[0])
    panel = lax.axis_index("blk")
    core = lax.rem(lax.axis_index("grp"), CORES)
    here = (lax.div(panel, XLO * SIDE), lax.rem(lax.div(panel, SIDE), XLO), lax.rem(panel, SIDE))
    n = 0
    for kind in range(2):
        for flip in range(CORES):
            for outer in OFFSETS:
                for j, inner in enumerate(OFFSETS):
                    dy, dz = (inner, outer) if kind == 0 else (outer, inner)
                    y = lax.rem(here[0] + dy + SIDE, SIDE)
                    z = lax.rem(here[2] + dz + SIDE, SIDE)
                    for k in range(XLO):
                        x = here[1] if k == 0 else 1 - here[1]
                        half = ((y * XLO + x) * SIDE + z) * 2 + (core if flip == 0 else 1 - core)
                        source = pieces[n].at[j * XLO + k]
                        first = half * HALF + (0 if kind == 0 else PART_A)
                        size = PART_A if kind == 0 else PART_B
                        pltpu.make_async_copy(
                            source.at[pl.ds(0, size)],
                            factors.at[pl.ds(pl.multiple_of(first, 16), size)],
                            sems.at[1],
                        ).start()
                        if kind == 0:
                            pltpu.make_async_copy(
                                source.at[pl.ds(PART_A, TAIL)], tails.at[half], sems.at[3]
                            ).start()
                n += 1
    conf_copy.start()
    conf[TILES] = jnp.zeros((BS, BS), BF)
    live = count[0]

    for b in range(UB):
        heads[b] = 0

    def tally(t, carry):
        b = users[t]
        heads[b] = heads[b] + 1
        return carry

    lax.fori_loop(0, live, tally, 0)
    ends = []
    begin = jnp.int32(0)
    for b in range(UB):
        size = heads[b]
        heads[b] = begin
        begin = begin + (size + GROUP - 1) // GROUP * GROUP
        ends.append(begin)
    batches = (ends[-1] + GROUP * BATCH - 1) // (GROUP * BATCH)

    def blank(s, carry):
        slots[s] = TILES
        return carry

    lax.fori_loop(0, batches * (GROUP * BATCH), blank, 0)

    def place(t, carry):
        b = users[t]
        s = heads[b]
        slots[s] = t
        heads[b] = s + 1
        return carry

    lax.fori_loop(0, live, place, 0)

    pltpu.make_async_copy(factors, factors, sems.at[1]).wait()
    pltpu.make_async_copy(tails, tails, sems.at[3]).wait()

    def level_step(h, carry):
        row = tails[h].astype(F32)[0:1, :]
        exposure[pl.ds(2 * h, 1), :] = row[:, :BS]
        exposure[pl.ds(2 * h + 1, 1), :] = row[:, BS:]
        return carry

    lax.fori_loop(0, TILES // 2, level_step, 0, unroll=8)

    gram[...] = gram_here[...] + gram_there[...]
    conf_copy.wait()

    def group_of(g):
        first = g * GROUP
        b = (
            (first >= ends[0]).astype(jnp.int32)
            + (first >= ends[1]).astype(jnp.int32)
            + (first >= ends[2]).astype(jnp.int32)
        )
        confs, parts, levels = [], [], []
        for j in range(GROUP):
            t = slots[first + j]
            item = items[jnp.minimum(t, TILES - 1)]
            confs.append(conf[t])
            parts.append(factors[pl.ds(pl.multiple_of(item * BS, BS), BS), :])
            levels.append(exposure[pl.ds(item, 1), :])
        rows = pl.ds(pl.multiple_of(b * BS, BS), BS)
        return rows, jnp.concatenate(confs, axis=1), jnp.concatenate(parts, axis=0), levels

    right[...] = jnp.zeros_like(right)

    def right_step(g):
        rows, weights, parts, _ = group_of(g)
        right[rows, :] += nn(weights, parts)

    def each_group(step):
        def batch(n, carry):
            for j in range(BATCH):
                step(n * BATCH + j)
            return carry

        lax.fori_loop(0, batches, batch, 0)

    each_group(right_step)

    def map_step(g):
        rows, weights, parts, levels = group_of(g)
        wide = weights.astype(F32)
        excess = jnp.where(wide > 0, wide - jnp.concatenate(levels, axis=1), 0.0)
        scores = nt(narrow[rows, :], parts)
        mapped[rows, :] += nn((excess * scores).astype(BF), parts)

    residual[...] = right[...]
    direction[...] = right[...]
    answer[...] = jnp.zeros_like(answer)
    norm = row_sum(right[...] * right[...])
    for step in range(STEPS):
        way = direction[...]
        narrow[...] = way.astype(BF)
        mapped[...] = way + jnp.dot(way, gram[...], precision=HIGH, preferred_element_type=F32)
        each_group(map_step)
        image = mapped[...]
        stride = norm / row_sum(way * image)
        answer[...] += stride * way
        if step < STEPS - 1:
            rest = residual[...] - stride * image
            residual[...] = rest
            norm_next = row_sum(rest * rest)
            direction[...] = rest + norm_next / norm * way
            norm = norm_next

    result = answer[...].astype(BF)
    out[...] = result

    for send, size, first in zip((send_0, send_1, send_2), ROWS, STARTS, strict=True):
        for b in range(UB):
            send[b * size : (b + 1) * size, :] = result[b * BS + first : b * BS + first + size, :]
        send[UB * size :, :] = tail_ref[...]
    gram_out[...] = tn(result, result)


def gram_kernel(*refs):
    parts_a, parts_b, out = refs[:SIDE], refs[SIDE : 2 * SIDE], refs[-1]
    out[...] = jnp.zeros_like(out)
    for n in range(SIDE):
        for m in range(SIDE):
            for k in range(XLO):
                first = parts_a[n][m * XLO + k]
                rows = jnp.concatenate([first[:PART_A], parts_b[m][n * XLO + k]], axis=0)
                weights = first[PART_A:].astype(F32)[0:1, :]
                scaled = rows.astype(F32).T * weights
                high = scaled.astype(BF)
                low = (scaled - high.astype(F32)).astype(BF)
                out[...] += nn(high, rows) + nn(low, rows)


def gram_half(parts_a, parts_b):
    vmem = pl.BlockSpec(memory_space=pltpu.VMEM)
    return pl.pallas_call(
        gram_kernel,
        out_shape=jax.ShapeDtypeStruct((RANK, RANK), F32),
        in_specs=[vmem] * (2 * SIDE),
        out_specs=vmem,
        compiler_params=pltpu.CompilerParams(vmem_limit_bytes=VMEM_BYTES),
        cost_estimate=pl.CostEstimate(flops=1_000_000_000, bytes_accessed=1_000_000, transcendentals=0),
        name="gram_half",
    )(*parts_a, *parts_b)


def user_half(items, users, count, grams, tail, conf, pieces):
    smem = pl.BlockSpec(memory_space=pltpu.SMEM)
    vmem = pl.BlockSpec(memory_space=pltpu.VMEM)
    far = pl.BlockSpec(memory_space=pl.ANY)
    wide = pltpu.VMEM((UB * BS, RANK), F32)
    return pl.pallas_call(
        user_kernel,
        out_shape=(
            jax.ShapeDtypeStruct((UB * BS, RANK), BF),
            *(jax.ShapeDtypeStruct((UB * size + TAIL, RANK), BF) for size in ROWS),
            jax.ShapeDtypeStruct((RANK, RANK), F32),
        ),
        in_specs=[smem, smem, smem, vmem, vmem, vmem, far] + [far] * len(pieces),
        out_specs=(vmem,) * 5,
        scratch_shapes=[
            pltpu.VMEM((TILES + 1, BS, BS), BF),
            pltpu.VMEM((TILES * BS, RANK), BF),
            pltpu.VMEM((TILES // 2, TAIL, RANK), BF),
            pltpu.VMEM((TILES, BS), F32),
            pltpu.SMEM((SLOTS,), jnp.int32),
            pltpu.SMEM((UB,), jnp.int32),
            pltpu.VMEM((RANK, RANK), F32),
            wide,
            wide,
            pltpu.VMEM((UB * BS, RANK), BF),
            wide,
            wide,
            wide,
            pltpu.SemaphoreType.DMA((4,)),
        ],
        compiler_params=pltpu.CompilerParams(vmem_limit_bytes=VMEM_BYTES),
        cost_estimate=pl.CostEstimate(flops=5_000_000_000, bytes_accessed=4_000_000, transcendentals=0),
        name="user_half",
    )(items, users, count, *grams, tail, conf, *pieces)


def select_kernel(*refs):
    planes = refs[: 3 * SIDE]
    outs = refs[3 * SIDE : 6 * SIDE]
    wide, blocks, sem = refs[6 * SIDE :]
    at, core = coordinates()
    for p, size in enumerate(ROWS):
        for j in range(SIDE):
            for k in range(SIDE):
                tail = planes[p * SIDE + j][k, UB * size : UB * size + TAIL, :BS].astype(F32)
                wide[p, j * SIDE + k, :] = tail[0, :].astype(jnp.int32)
    copy = pltpu.make_async_copy(wide, blocks, sem)
    copy.start()
    copy.wait()
    for p, size in enumerate(ROWS):
        for m in range(MESSAGES):
            there = dict(at)
            there[ORDERS[p][2]] = (at[ORDERS[p][2]] - OFFSETS[m // CORES]) & 3
            owner = join_place(there, core ^ (m % CORES))
            for j in range(SIDE):
                for k in range(SIDE):
                    block = blocks[p, j * SIDE + k, owner]
                    rows = pl.ds(pl.multiple_of(block * size, 16), size)
                    outs[p * SIDE + m // CORES][m % CORES, j * SIDE + k] = planes[p * SIDE + j][k, rows, :]


def select(planes):
    vmem = pl.BlockSpec(memory_space=pltpu.VMEM)
    shapes = [
        jax.ShapeDtypeStruct((CORES, SIDE * SIDE, size, RANK), BF) for size in ROWS for _ in OFFSETS
    ]
    return pl.pallas_call(
        select_kernel,
        out_shape=shapes,
        in_specs=[vmem] * len(planes),
        out_specs=[vmem] * len(shapes),
        scratch_shapes=[
            pltpu.VMEM((3, SIDE * SIDE, BS), jnp.int32),
            pltpu.SMEM((3, SIDE * SIDE, BS), jnp.int32),
            pltpu.SemaphoreType.DMA,
        ],
        compiler_params=pltpu.CompilerParams(vmem_limit_bytes=VMEM_BYTES),
        cost_estimate=pl.CostEstimate(flops=0, bytes_accessed=16_000_000, transcendentals=0),
        name="select",
    )(*planes)


ITEM_GROUP = 16
CHUNKS = TILES // ITEM_GROUP


def item_kernel(conf_hbm, exposure, user_gram, *refs):
    messages, refs = refs[: 3 * MESSAGES], refs[3 * MESSAGES :]
    out, conf, rows_0, rows_1, rows_2, mapped, narrow, slots, sems = refs
    parts = (rows_0, rows_1, rows_2)
    for p in range(3):
        for m in range(MESSAGES):
            message = messages[p * MESSAGES + m]
            pltpu.make_async_copy(
                message if m % CORES else message.at[0],
                parts[p].at[pl.ds(m * SIDE * SIDE, SIDE * SIDE)],
                sems.at[p],
            ).start()
    conf_copy = pltpu.make_async_copy(conf_hbm, conf, sems.at[3])
    conf_copy.start()
    here, core = coordinates()

    def slot_step(place, carry):
        there, other = split_place(place)
        steps = {axis: offset_index(there[axis], here[axis]) for axis in here}
        for p, (first, second, third) in enumerate(ORDERS):
            message = steps[third] * CORES + (other ^ core)
            slots[p, place] = (message * SIDE + steps[second]) * SIDE + steps[first]
        return carry

    lax.fori_loop(0, TILES, slot_step, 0)
    level = jnp.broadcast_to(exposure[...], (BS, BS)).T
    level_wide = jnp.concatenate([level] * ITEM_GROUP, axis=1)
    level_rank = jnp.concatenate([level] * (RANK // BS), axis=1)

    def chunk_of(c):
        weights = jnp.concatenate([conf[c * ITEM_GROUP + j] for j in range(ITEM_GROUP)], axis=1)
        part = jnp.concatenate(
            [parts[p][slots[p, c * ITEM_GROUP + j]] for j in range(ITEM_GROUP) for p in range(3)],
            axis=0,
        )
        return weights, part

    def right_step(c, carry):
        weights, part = chunk_of(c)
        mapped[...] += nn(weights, part)
        return carry

    def map_step(c, carry):
        weights, part = chunk_of(c)
        wide = weights.astype(F32)
        excess = jnp.where(wide > 0, wide - level_wide, 0.0)
        scores = nt(narrow[...], part)
        mapped[...] += nn((excess * scores).astype(BF), part)
        return carry

    mapped[...] = jnp.zeros_like(mapped)
    for p in range(3):
        pltpu.make_async_copy(parts[p], parts[p], sems.at[p]).wait()
    conf_copy.wait()
    lax.fori_loop(0, CHUNKS, right_step, 0, unroll=4)
    residual = mapped[...]
    way = residual
    answer = jnp.zeros_like(residual)
    norm = row_sum(residual * residual)
    for step in range(STEPS):
        narrow[...] = way.astype(BF)
        term = jnp.dot(way, user_gram[...], precision=HIGH, preferred_element_type=F32)
        mapped[...] = way + level_rank * term
        lax.fori_loop(0, CHUNKS, map_step, 0, unroll=4)
        image = mapped[...]
        stride = norm / row_sum(way * image)
        answer = answer + stride * way
        if step < STEPS - 1:
            residual = residual - stride * image
            norm_next = row_sum(residual * residual)
            way = residual + norm_next / norm * way
            norm = norm_next
    out[...] = (answer * (float(TILES) ** 0.5)).astype(BF)


def item_half(conf, exposure, user_gram, messages):
    vmem = pl.BlockSpec(memory_space=pltpu.VMEM)
    far = pl.BlockSpec(memory_space=pl.ANY)
    return pl.pallas_call(
        item_kernel,
        out_shape=jax.ShapeDtypeStruct((BS, RANK), BF),
        in_specs=[far, vmem, vmem] + [far] * len(messages),
        out_specs=vmem,
        scratch_shapes=[
            pltpu.VMEM((TILES, BS, BS), BF),
            *(pltpu.VMEM((TILES, size, RANK), BF) for size in ROWS),
            pltpu.VMEM((BS, RANK), F32),
            pltpu.VMEM((BS, RANK), BF),
            pltpu.SMEM((3, TILES), jnp.int32),
            pltpu.SemaphoreType.DMA((4,)),
        ],
        compiler_params=pltpu.CompilerParams(vmem_limit_bytes=VMEM_BYTES),
        name="item_half",
    )(conf, exposure, user_gram, *messages)


def exchange(values, axes):
    return lax.all_to_all(values, axes, split_axis=0, concat_axis=0, tiled=True)


def sum_axis(half, axis):
    near, far, across = (fetch(half, **{axis: d}) for d in OFFSETS[1:])
    return (half + across) + (near + far)


def sum_chip(values, core):
    rows = values.shape[0] // CORES
    first = values[:rows]
    second = values[rows:]
    return jnp.where(core == 0, first, second) + fetch(
        jnp.where(core == 0, second, first), flip=1
    )


def sum_rest(half, core):
    half = sum_axis(sum_axis(half, "dy"), "dz")
    other = fetch(half, flip=1)
    return jnp.concatenate(
        [jnp.where(core == 0, half, other), jnp.where(core == 0, other, half)], axis=0
    )


def gather_line(near, far, across, axis, here):
    near = fetch(near, **{axis: 1})
    far = fetch(far, **{axis: -1})
    near, across = lax.optimization_barrier((near, across))
    return [here, near, far, fetch(across, **{axis: 2})]


def body(item_factors, exposure, confidence, tile_items, tile_users, tile_count):
    conf_tiles = confidence[0]
    items = tile_items[0]
    users = tile_users[0]
    core = lax.rem(lax.axis_index("grp"), CORES)
    mine = lax.dynamic_slice_in_dim(item_factors, core * HALF, HALF)
    level = jnp.pad(
        lax.dynamic_slice_in_dim(exposure, core * HALF, HALF)[None], ((0, TAIL - 1), (0, 0))
    )
    part_a = jnp.concatenate([mine[:PART_A], level], axis=0)
    paired = jnp.zeros((TILES,), jnp.int32).at[items].set(users).astype(BF)
    tail = jnp.pad(paired[None], ((0, TAIL - 1), (0, RANK - TILES)))
    part_b = mine[PART_A:]
    part_a = jnp.stack([part_a, fetch(part_a, dx=1)])
    part_b = jnp.stack([part_b, fetch(part_b, dx=-1)])
    line_a = jnp.concatenate([part_a] + [fetch(part_a, dy=d) for d in OFFSETS[1:]], axis=0)
    line_b = jnp.concatenate([part_b] + [fetch(part_b, dz=d) for d in OFFSETS[1:]], axis=0)
    send_conf = send_conf_of(items, tile_count, conf_tiles)
    line_a, line_b = lax.optimization_barrier((line_a, line_b))
    full_a = [line_a] + [fetch(line_a, dz=d) for d in OFFSETS[1:]]
    full_b = [line_b] + [fetch(line_b, dy=d) for d in OFFSETS[1:]]
    full_a[1:], full_b[1:], send_conf = lax.optimization_barrier(
        (full_a[1:], full_b[1:], send_conf)
    )
    got_conf = exchange(send_conf, BOTH)
    pieces = (
        full_a + [fetch(v, flip=1) for v in full_a]
        + full_b + [fetch(v, flip=1) for v in full_b]
    )
    gram_own = gram_half(full_a, full_b)
    user_factors, *sends, local_gram = user_half(
        items, users, tile_count, (gram_own, fetch(gram_own, flip=1)), tail, conf_tiles, pieces
    )
    half_gram = sum_axis(sum_chip(local_gram, core), "dx")
    sends, got_conf, half_gram = lax.optimization_barrier((sends, got_conf, half_gram))
    moved = {(d, p): fetch(sends[p], **{ORDERS[p][0]: d}) for d in OFFSETS[1:] for p in range(3)}
    lines = [jnp.stack([sends[p]] + [moved[d, p] for d in OFFSETS[1:]]) for p in range(3)]
    lines = lax.optimization_barrier(lines)
    planes = []
    for p in range(3):
        planes += gather_line(lines[p], lines[p], lines[p], ORDERS[p][1], lines[p])
    planes, half_gram = lax.optimization_barrier((planes, half_gram))
    chosen = select(planes)
    arrived = {}
    for p in range(3):
        here, near, far, across = chosen[p * SIDE : (p + 1) * SIDE]
        for n, v in enumerate(gather_line(near, far, across, ORDERS[p][2], here)):
            arrived[p, n] = (v, fetch(v[1], flip=1))
    messages = [arrived[p, n][f] for p in range(3) for n in range(SIDE) for f in range(CORES)]
    user_gram = sum_rest(half_gram, core) * (1.0 / (UB * BS))
    own = lax.dynamic_slice_in_dim(exposure, lax.axis_index("grp") * BS, BS)
    item_update = item_half(got_conf, own.astype(F32).reshape(1, BS), user_gram, messages)
    return user_factors, item_update, user_gram


def solution(mesh):
    placed = (
        P("blk", None),
        P("blk"),
        P(BOTH, None, None, None),
        P(BOTH, None),
        P(BOTH, None),
        P(BOTH),
    )
    return jax.shard_map(
        body,
        mesh=mesh,
        in_specs=placed,
        out_specs=(P(BOTH, None), P(BOTH, None), P()),
        check_vma=False,
    )
```
